32 devices in a mesh: group: 8 (over z, core), sub: 4 (over y, x).
Axes of the slice: x: 2, y: 2, z: 4, core: 2. Of those that a mesh axis runs over, the one named last changes fastest.
Arguments:
- points: bfloat16 [32768, 768], P(('group', 'sub')), may hold values from -6 to 6
- anchors: bfloat16 [256, 768], replicated, may hold values from -6 to 6
- neighbours: int32 [64, 4], P(('group', 'sub')), may hold values from 0 to 63, as said below
Outputs:
- near_blocks: float32 [32768, 4, 512], P(('group', 'sub'))
- leaf_basis: bfloat16 [32768, 256], P(('group', 'sub'))
- transfer: float32 [32, 2, 256, 256], P(('group', 'sub'))
- coupling: float32 [32, 2, 256, 256], P(('group', 'sub'))
The draws below stay inside these ranges and needn't reach their ends.
Inputs may be any that keep to these rules, and one draw needn't show every extreme that they name: Each leaf's 4 neighbours are different leaves at cyclic distance 1, 2 or 3 from it in the order of leaf numbers modulo 64.
All inputs are finite; a program needn't handle non-finite values.
Results may differ from the reference program's by a relative error of at most 0.0077.
Values may be sent and summed in bfloat16 or wider, within the bound.
A program may use at most 128 MiB of HBM per device.

```python
import math
import jax
import jax.numpy as jnp
from jax import lax

D = 768
R = 256
LEAF = 512
NBR = 4
LEAVES_DEV = 2
LEAVES = 64
POINTS = 32768
LEVELS = 2
N_GROUP = 8
N_SUB = 4
DEVICES = 32


def draw_neighbours(key, part):
    key = jax.random.fold_in(key, 11)
    scores = jax.random.randint(key, (LEAVES, 6), 0, 1 << 20) * 8 + jnp.arange(6, dtype=jnp.int32)[None, :]
    chosen = jnp.sort(jnp.argsort(scores, axis=1)[:, :NBR].astype(jnp.int32), axis=1)
    table = jnp.array([-3, -2, -1, 1, 2, 3], dtype=jnp.int32)
    offsets = jnp.take(table, chosen)
    own = jnp.arange(LEAVES, dtype=jnp.int32)[:, None]
    return jnp.remainder(own + offsets, LEAVES).astype(jnp.int32)


def levels(key, shape, split, smallest, largest):
    gain = 1.0
    for axis_at, shards_of in split:
        heights = jax.random.uniform(jax.random.fold_in(jax.random.fold_in(key, 6), axis_at), (shards_of,), jnp.float32, smallest / len(split), largest / len(split))
        gain = gain * jnp.repeat(jnp.exp(heights), shape[axis_at] // shards_of).reshape((-1,) + (1,) * (len(shape) - 1 - axis_at))
    return gain


def centred(key, extent, deviation, limit, cuts=(), kind=jnp.bfloat16):
    factor_of = levels(key, extent, cuts, -0.22, 0.18) if cuts else 1.0
    values = jax.random.normal(key, extent, jnp.float32) * deviation * factor_of
    return jnp.minimum(jnp.maximum(values, -limit), limit).astype(kind)


def setup_inputs(seed: int = 0) -> dict:
    key_list = jax.random.split(jax.random.key(seed), 4)
    return {
        "points": centred(key_list[0], (POINTS, D), 1.0, 6.0, ((0, 32),)),
        "anchors": centred(key_list[1], (R, D), 1.0, 6.0),
        "neighbours": draw_neighbours(jax.random.fold_in(key_list[3], 71), 0),
    }


def unit_rows(values):
    wide = values.astype(jnp.float32)
    scale = lax.rsqrt(lax.optimization_barrier(jnp.sum(wide * wide, axis=-1, keepdims=True)) + 1e-06)
    return (wide * scale).astype(jnp.bfloat16)

def lower_solve(factor, right):
    return lax.linalg.triangular_solve(factor, right, left_side=True, lower=True)

def swap_last(matrix):
    return jnp.swapaxes(matrix, -1, -2)

def reference(points, anchors, neighbours):
    beta = 0.5 * math.sqrt(D)
    unit = unit_rows(points)
    anchor_unit = unit_rows(anchors)
    leaves = unit.reshape(LEAVES, LEAF, D)

    def near_leaf(inputs):
        rows, picks = inputs
        cols = jnp.take(leaves, picks, axis=0)
        scores = jnp.einsum('pd,kqd->pkq', rows.astype(jnp.float32), cols.astype(jnp.float32))
        return jnp.exp(beta * scores)
    near_blocks = lax.map(near_leaf, (leaves, neighbours)).reshape(POINTS, NBR, LEAF)
    sketch = jnp.exp(beta * jnp.dot(unit.astype(jnp.float32), anchor_unit.T.astype(jnp.float32), preferred_element_type=jnp.float32))
    sketch = sketch.reshape(LEAVES, LEAF, R)
    grams = jnp.einsum('lpr,lps->lrs', sketch, sketch, precision=lax.Precision.HIGHEST) / LEAF
    factors = jnp.linalg.cholesky(grams)
    basis = swap_last(lower_solve(factors, swap_last(sketch)))
    leaf_basis = basis.reshape(POINTS, R).astype(jnp.bfloat16)
    dev_grams = lax.optimization_barrier(jnp.sum(grams.reshape(DEVICES, LEAVES_DEV, R, R), axis=1)) / LEAVES_DEV
    nodes = dev_grams.reshape(N_GROUP, N_SUB, R, R)
    transfers = []
    couplings = []
    for level in range(LEVELS):
        count = nodes.shape[1]
        pairs = nodes.reshape(N_GROUP, count // 2, 2, R, R)
        left = pairs[:, :, 0]
        right = pairs[:, :, 1]
        parent = (left + right) * 0.5
        left_factor = jnp.linalg.cholesky(left)
        right_factor = jnp.linalg.cholesky(right)
        parent_factor = jnp.linalg.cholesky(parent)
        left_transfer = swap_last(lower_solve(parent_factor, left_factor))
        right_transfer = swap_last(lower_solve(parent_factor, right_factor))
        left_coupling = lower_solve(left_factor, right_factor)
        right_coupling = lower_solve(right_factor, left_factor)
        both_transfer = jnp.stack([left_transfer, right_transfer], axis=2).reshape(N_GROUP, count, R, R)
        both_coupling = jnp.stack([left_coupling, right_coupling], axis=2).reshape(N_GROUP, count, R, R)
        transfers.append(jnp.repeat(both_transfer, 2 ** level, axis=1).reshape(DEVICES, R, R))
        couplings.append(jnp.repeat(both_coupling, 2 ** level, axis=1).reshape(DEVICES, R, R))
        nodes = parent
    transfer = jnp.stack(transfers, axis=1)
    coupling = jnp.stack(couplings, axis=1)
    return (near_blocks, leaf_basis, transfer, coupling)
```

```python
import functools
import math

import jax
import jax.numpy as jnp
from jax import lax
from jax.experimental import pallas as pl
from jax.experimental.pallas import tpu as pltpu
from jax.sharding import PartitionSpec as P

LEAF = 512
PANEL = 32
HIGHEST = lax.Precision.HIGHEST


def from_behind(value, axis, steps):
    count = lax.axis_size(axis)
    pairs = [(source, (source + steps) % count) for source in range(count)]
    return lax.ppermute(value, axis, pairs)


def from_partner(block, axis, stride):
    count = lax.axis_size(axis)
    route = []
    for low in range(count):
        high = low | 1 << stride
        if high != low and high < count:
            route += [(low, high), (high, low)]
    return lax.ppermute(block, axis, route)


def unit_rows(values):
    wide = values.astype(jnp.float32)
    scale = lax.rsqrt(jnp.sum(wide * wide, axis=-1, keepdims=True) + 1e-06)
    return (wide * scale).astype(jnp.bfloat16)


def split3(x):
    a = x.astype(jnp.bfloat16)
    rest = x - a.astype(jnp.float32)
    b = rest.astype(jnp.bfloat16)
    c = (rest - b.astype(jnp.float32)).astype(jnp.bfloat16)
    return a, b, c


def factor_kernel(count, rank, grams_ref, upper_ref, inverse_ref, work, *blocks):
    b = PANEL
    eye_row = lax.broadcasted_iota(jnp.int32, (rank, rank), 0)
    eye_col = lax.broadcasted_iota(jnp.int32, (rank, rank), 1)
    eye = jnp.where(eye_row == eye_col, 1.0, 0.0).astype(jnp.float32)
    for m in range(count):
        work[m, :, :rank] = grams_ref[m]
        work[m, :, rank:] = eye
    for block in blocks:
        block[...] = jnp.ones_like(block)
    lane = lax.broadcasted_iota(jnp.int32, (b, 128), 1)
    row = lax.broadcasted_iota(jnp.int32, (b, 128), 0)
    unit_part = jnp.where(lane == row + b, 1.0, 0.0).astype(jnp.float32)
    panel_row = lax.broadcasted_iota(jnp.int32, (b, rank), 0)
    panel_col = lax.broadcasted_iota(jnp.int32, (b, rank), 1)

    def panel(step, carry):
        start = pl.multiple_of(step * b, b)
        for m in range(count):
            rows = work[m, pl.ds(start, b), :rank]
            rolled = pltpu.roll(rows, rank - start, 1)[:, :128]
            blocks[m // 8][pl.ds(m % 8, b, stride=8), :] = jnp.where(lane < b, rolled, unit_part)
        for block in blocks:
            v = [block[r * 8:(r + 1) * 8, :] for r in range(b)]
            for k in range(b):
                pivot = jnp.broadcast_to(v[k][:, k:k + 1], (8, 128))
                scaled = v[k] * (1.0 / pivot)
                for i in range(k + 1, b):
                    v[i] = v[i] - jnp.broadcast_to(v[k][:, i:i + 1], (8, 128)) * scaled
                block[k * 8:(k + 1) * 8, :] = v[k] * lax.rsqrt(pivot)
        for m in range(count):
            small = blocks[m // 8][pl.ds(m % 8, b, stride=8), :][:, b:2 * b]
            reduced = jnp.dot(small, work[m, pl.ds(start, b), :], precision=HIGHEST, preferred_element_type=jnp.float32)
            left = jnp.where(panel_col >= start + panel_row, reduced[:, :rank], 0.0)
            work[m, pl.ds(start, b), :rank] = left
            work[m, pl.ds(start, b), rank:] = reduced[:, rank:]
            full = jnp.concatenate([left, reduced[:, rank:]], axis=1)
            y1, y2, y3 = split3(full)
            x1, x2, x3 = split3(jnp.where(panel_col >= start + b, left, 0.0))
            lhs = jnp.concatenate([x1, x1, x2, x2, x1, x3], axis=0)
            rhs = jnp.concatenate([y1, y2, y1, y2, y3, y1], axis=0)
            work[m] = work[m] - lax.dot_general(lhs, rhs, (((0,), (0,)), ((), ())), preferred_element_type=jnp.float32)
        return carry

    lax.fori_loop(0, rank // b, panel, 0)
    for m in range(count):
        upper_ref[m] = work[m, :, :rank]
        inverse_ref[m] = work[m, :, rank:]


def factors_of(grams):
    count, rank, _ = grams.shape
    shape = jax.ShapeDtypeStruct((count, rank, rank), jnp.float32)
    vmem = pl.BlockSpec(memory_space=pltpu.VMEM)
    return pl.pallas_call(
        functools.partial(factor_kernel, count, rank),
        out_shape=(shape, shape),
        in_specs=[vmem],
        out_specs=(vmem, vmem),
        scratch_shapes=[pltpu.VMEM((count, rank, 2 * rank), jnp.float32)]
        + [pltpu.VMEM((8 * PANEL, 128), jnp.float32)] * ((count + 7) // 8),
        compiler_params=pltpu.CompilerParams(vmem_limit_bytes=40 << 20),
        cost_estimate=pl.CostEstimate(flops=40_000_000_000, bytes_accessed=8_000_000, transcendentals=0),
        name="factor",
    )(grams)


def near_kernel(beta, picks_ref, *refs):
    *parts, rows_ref, out_ref, window, sems = refs
    leaf = pl.program_id(0)

    @pl.when((leaf == 0) & (pl.program_id(1) == 0))
    def _():
        at = 0
        copies = []
        for n, part in enumerate(parts):
            size = part.shape[0]
            copies.append(pltpu.make_async_copy(part, window.at[pl.ds(at, size)], sems.at[n]))
            at += size
        for copy in copies:
            copy.start()
        for copy in copies:
            copy.wait()

    rows = rows_ref[0]
    for j in range(out_ref.shape[1]):
        cols = window[picks_ref[leaf, j]]
        scores = lax.dot_general(rows, cols, (((1,), (1,)), ((), ())), preferred_element_type=jnp.float32)
        out_ref[:, j, :] = jnp.exp(beta * scores)


def near_field(parts, leaves, picks, beta):
    leaves_dev, leaf, width = leaves.shape
    nbr = picks.shape[1]
    chunk = 256
    steps = leaf // chunk
    total = sum(part.shape[0] for part in parts)
    return pl.pallas_call(
        functools.partial(near_kernel, beta),
        out_shape=jax.ShapeDtypeStruct((leaves_dev * leaf, nbr, leaf), jnp.float32),
        grid_spec=pltpu.PrefetchScalarGridSpec(
            num_scalar_prefetch=1,
            grid=(leaves_dev, steps),
            in_specs=[pl.BlockSpec(memory_space=pl.ANY)] * len(parts)
            + [pl.BlockSpec((1, chunk, width), lambda a, c, p: (a, c, 0))],
            out_specs=pl.BlockSpec((chunk, nbr, leaf), lambda a, c, p: (a * steps + c, 0, 0)),
            scratch_shapes=[
                pltpu.VMEM((total, leaf, width), jnp.bfloat16),
                pltpu.SemaphoreType.DMA((len(parts),)),
            ],
        ),
        compiler_params=pltpu.CompilerParams(vmem_limit_bytes=40 << 20),
        cost_estimate=pl.CostEstimate(flops=4_000_000_000, bytes_accessed=16_000_000, transcendentals=2_000_000),
        name="near",
    )(picks, *parts, leaves)


def shards(points, anchors, neighbours):
    leaves_dev = neighbours.shape[0]
    width = points.shape[1]
    rank = anchors.shape[0]
    beta = 0.5 * math.sqrt(width)
    unit = unit_rows(points)
    anchor_unit = unit_rows(anchors)
    leaves = unit.reshape(leaves_dev, LEAF, width)
    reach = 3
    lower_parts = []
    upper_parts = []
    plan = []
    for step in range(1, (reach + leaves_dev - 1) // leaves_dev + 1):
        count = min(leaves_dev, reach - (step - 1) * leaves_dev)
        plan.append((leaves[leaves_dev - count :], step))
        plan.append((leaves[:count], -step))
    for piece, step in plan:
        got = from_behind(piece, ("group", "sub"), step)
        if step > 0:
            lower_parts.insert(0, got)
        else:
            upper_parts.append(got)

    sketch = jnp.exp(beta * jnp.dot(unit, anchor_unit.T, preferred_element_type=jnp.float32))
    sketch = sketch.reshape(leaves_dev, LEAF, rank)
    grams = jnp.einsum("lpr,lps->lrs", sketch, sketch, precision=HIGHEST) / LEAF
    node = jnp.sum(grams, axis=0) / leaves_dev
    levels = lax.axis_size("sub").bit_length() - 1
    stack = [grams[leaf] for leaf in range(leaves_dev)] + [node]
    for level in range(levels):
        partner = from_partner(node, "sub", level)
        node = (node + partner) * 0.5
        stack += [partner, node]
    upper, inverse = factors_of(jnp.stack(stack, axis=0))
    basis = jnp.einsum("lpr,lsr->lps", sketch, inverse[:leaves_dev], precision=HIGHEST)
    leaf_basis = basis.reshape(leaves_dev * LEAF, rank).astype(jnp.bfloat16)
    own = slice(leaves_dev, leaves_dev + 2 * levels, 2)
    sibling = slice(leaves_dev + 1, leaves_dev + 1 + 2 * levels, 2)
    parent = slice(leaves_dev + 2, leaves_dev + 2 + 2 * levels, 2)
    transfer = jnp.einsum("tij,tkj->tik", upper[own], inverse[parent], precision=HIGHEST)[None]
    coupling = jnp.einsum("tij,tkj->tik", inverse[own], upper[sibling], precision=HIGHEST)[None]

    total_leaves = leaves_dev * lax.axis_size(("group", "sub"))
    first_leaf = lax.axis_index(("group", "sub")) * leaves_dev
    local = jnp.arange(leaves_dev, dtype=jnp.int32)[:, None]
    offsets = jnp.remainder(neighbours - first_leaf - local + reach, total_leaves) - reach
    picks = reach + local + offsets
    near_blocks = near_field(lower_parts + [leaves] + upper_parts, leaves, picks, beta)
    return (near_blocks, leaf_basis, transfer, coupling)


def solution(mesh):
    return jax.shard_map(
        shards,
        mesh=mesh,
        in_specs=(P(("group", "sub"), None), P(), P(("group", "sub"), None)),
        out_specs=(
            P(("group", "sub"), None, None),
            P(("group", "sub"), None),
            P(("group", "sub"), None, None, None),
            P(("group", "sub"), None, None, None),
        ),
        check_vma=False,
    )
```

```python
import functools
import math

import jax
import jax.numpy as jnp
from jax import lax
from jax.experimental import pallas as pl
from jax.experimental.pallas import tpu as pltpu
from jax.sharding import PartitionSpec as P

LEAF = 512
PANEL = 32
HIGHEST = lax.Precision.HIGHEST


def from_behind(value, axis, steps):
    count = lax.axis_size(axis)
    pairs = [(source, (source + steps) % count) for source in range(count)]
    return lax.ppermute(value, axis, pairs)


def from_partner(block, axis, stride):
    count = lax.axis_size(axis)
    route = []
    for low in range(count):
        high = low | 1 << stride
        if high != low and high < count:
            route += [(low, high), (high, low)]
    return lax.ppermute(block, axis, route)


def unit_rows(values):
    wide = values.astype(jnp.float32)
    scale = lax.rsqrt(jnp.sum(wide * wide, axis=-1, keepdims=True) + 1e-06)
    return (wide * scale).astype(jnp.bfloat16)


def split3(x):
    a = x.astype(jnp.bfloat16)
    rest = x - a.astype(jnp.float32)
    b = rest.astype(jnp.bfloat16)
    c = (rest - b.astype(jnp.float32)).astype(jnp.bfloat16)
    return a, b, c


def factor_kernel(count, rank, grams_ref, upper_ref, inverse_ref, work, *blocks):
    b = PANEL
    eye_row = lax.broadcasted_iota(jnp.int32, (rank, rank), 0)
    eye_col = lax.broadcasted_iota(jnp.int32, (rank, rank), 1)
    eye = jnp.where(eye_row == eye_col, 1.0, 0.0).astype(jnp.float32)
    for m in range(count):
        work[m, :, :rank] = grams_ref[m]
        work[m, :, rank:] = eye
    for block in blocks:
        block[...] = jnp.ones_like(block)
    lane = lax.broadcasted_iota(jnp.int32, (b, 128), 1)
    row = lax.broadcasted_iota(jnp.int32, (b, 128), 0)
    unit_part = jnp.where(lane == row + b, 1.0, 0.0).astype(jnp.float32)
    panel_row = lax.broadcasted_iota(jnp.int32, (b, rank), 0)
    panel_col = lax.broadcasted_iota(jnp.int32, (b, rank), 1)

    def panel(step, carry):
        start = pl.multiple_of(step * b, b)
        for m in range(count):
            rows = work[m, pl.ds(start, b), :rank]
            rolled = pltpu.roll(rows, rank - start, 1)[:, :128]
            blocks[m // 8][pl.ds(m % 8, b, stride=8), :] = jnp.where(lane < b, rolled, unit_part)
        for block in blocks:
            v = [block[r * 8:(r + 1) * 8, :] for r in range(b)]
            for k in range(b):
                pivot = jnp.broadcast_to(v[k][:, k:k + 1], (8, 128))
                scaled = v[k] * (1.0 / pivot)
                for i in range(k + 1, b):
                    v[i] = v[i] - jnp.broadcast_to(v[k][:, i:i + 1], (8, 128)) * scaled
                block[k * 8:(k + 1) * 8, :] = v[k] * lax.rsqrt(pivot)
        for m in range(count):
            small = blocks[m // 8][pl.ds(m % 8, b, stride=8), :][:, b:2 * b]
            reduced = jnp.dot(small, work[m, pl.ds(start, b), :], precision=HIGHEST, preferred_element_type=jnp.float32)
            left = jnp.where(panel_col >= start + panel_row, reduced[:, :rank], 0.0)
            work[m, pl.ds(start, b), :rank] = left
            work[m, pl.ds(start, b), rank:] = reduced[:, rank:]
            full = jnp.concatenate([left, reduced[:, rank:]], axis=1)
            y1, y2, y3 = split3(full)
            x1, x2, x3 = split3(jnp.where(panel_col >= start + b, left, 0.0))
            lhs = jnp.concatenate([x1, x1, x2, x2, x1, x3], axis=0)
            rhs = jnp.concatenate([y1, y2, y1, y2, y3, y1], axis=0)
            work[m] = work[m] - lax.dot_general(lhs, rhs, (((0,), (0,)), ((), ())), preferred_element_type=jnp.float32)
        return carry

    lax.fori_loop(0, rank // b, panel, 0)
    for m in range(count):
        upper_ref[m] = work[m, :, :rank]
        inverse_ref[m] = work[m, :, rank:]


def factors_of(grams):
    count, rank, _ = grams.shape
    shape = jax.ShapeDtypeStruct((count, rank, rank), jnp.float32)
    vmem = pl.BlockSpec(memory_space=pltpu.VMEM)
    return pl.pallas_call(
        functools.partial(factor_kernel, count, rank),
        out_shape=(shape, shape),
        in_specs=[vmem],
        out_specs=(vmem, vmem),
        scratch_shapes=[pltpu.VMEM((count, rank, 2 * rank), jnp.float32)]
        + [pltpu.VMEM((8 * PANEL, 128), jnp.float32)] * ((count + 7) // 8),
        compiler_params=pltpu.CompilerParams(vmem_limit_bytes=40 << 20),
        cost_estimate=pl.CostEstimate(flops=40_000_000_000, bytes_accessed=8_000_000, transcendentals=0),
        name="factor",
    )(grams)


def near_kernel(beta, picks_ref, *refs):
    *parts, rows_ref, out_ref, window, sems = refs
    leaf = pl.program_id(0)

    @pl.when((leaf == 0) & (pl.program_id(1) == 0))
    def _():
        at = 0
        copies = []
        for n, part in enumerate(parts):
            size = part.shape[0]
            copies.append(pltpu.make_async_copy(part, window.at[pl.ds(at, size)], sems.at[n]))
            at += size
        for copy in copies:
            copy.start()
        for copy in copies:
            copy.wait()

    rows = rows_ref[0]
    for j in range(out_ref.shape[1]):
        cols = window[picks_ref[leaf, j]]
        scores = lax.dot_general(rows, cols, (((1,), (1,)), ((), ())), preferred_element_type=jnp.float32)
        out_ref[:, j, :] = jnp.exp(beta * scores)


def near_field(parts, leaves, picks, beta):
    leaves_dev, leaf, width = leaves.shape
    nbr = picks.shape[1]
    chunk = 256
    steps = leaf // chunk
    total = sum(part.shape[0] for part in parts)
    return pl.pallas_call(
        functools.partial(near_kernel, beta),
        out_shape=jax.ShapeDtypeStruct((leaves_dev * leaf, nbr, leaf), jnp.float32),
        grid_spec=pltpu.PrefetchScalarGridSpec(
            num_scalar_prefetch=1,
            grid=(leaves_dev, steps),
            in_specs=[pl.BlockSpec(memory_space=pl.ANY)] * len(parts)
            + [pl.BlockSpec((1, chunk, width), lambda a, c, p: (a, c, 0))],
            out_specs=pl.BlockSpec((chunk, nbr, leaf), lambda a, c, p: (a * steps + c, 0, 0)),
            scratch_shapes=[
                pltpu.VMEM((total, leaf, width), jnp.bfloat16),
                pltpu.SemaphoreType.DMA((len(parts),)),
            ],
        ),
        compiler_params=pltpu.CompilerParams(vmem_limit_bytes=40 << 20),
        cost_estimate=pl.CostEstimate(flops=4_000_000_000, bytes_accessed=16_000_000, transcendentals=2_000_000),
        name="near",
    )(picks, *parts, leaves)


def shards(points, anchors, neighbours):
    leaves_dev = neighbours.shape[0]
    width = points.shape[1]
    rank = anchors.shape[0]
    beta = 0.5 * math.sqrt(width)
    unit = unit_rows(points)
    anchor_unit = unit_rows(anchors)
    leaves = unit.reshape(leaves_dev, LEAF, width)
    reach = 3
    plan = []
    for step in range(1, (reach + leaves_dev - 1) // leaves_dev + 1):
        count = min(leaves_dev, reach - (step - 1) * leaves_dev)
        plan.append((leaves[leaves_dev - count :], step))
        plan.append((leaves[:count], -step))
    got = {}
    for piece, step in plan:
        if abs(step) > 1:
            got[step] = from_behind(piece, ("group", "sub"), step)

    sketch = jnp.exp(beta * jnp.dot(unit, anchor_unit.T, preferred_element_type=jnp.float32))
    sketch = sketch.reshape(leaves_dev, LEAF, rank)
    grams = jnp.einsum("lpr,lps->lrs", sketch, sketch, precision=HIGHEST) / LEAF
    node = jnp.sum(grams, axis=0) / leaves_dev
    levels = lax.axis_size("sub").bit_length() - 1
    stack = [grams[leaf] for leaf in range(leaves_dev)] + [node]
    for level in range(levels):
        partner = from_partner(node, "sub", level)
        node = (node + partner) * 0.5
        stack += [partner, node]
    near_pieces = [(piece, step) for piece, step in plan if abs(step) == 1]
    held, stack = lax.optimization_barrier(([piece for piece, _ in near_pieces], stack))
    for piece, (_, step) in zip(held, near_pieces):
        got[step] = from_behind(piece, ("group", "sub"), step)
    lower_parts = [got[step] for step in sorted(got, reverse=True) if step > 0]
    upper_parts = [got[step] for step in sorted(got, reverse=True) if step < 0]
    upper, inverse = factors_of(jnp.stack(stack, axis=0))
    basis = jnp.einsum("lpr,lsr->lps", sketch, inverse[:leaves_dev], precision=HIGHEST)
    leaf_basis = basis.reshape(leaves_dev * LEAF, rank).astype(jnp.bfloat16)
    own = slice(leaves_dev, leaves_dev + 2 * levels, 2)
    sibling = slice(leaves_dev + 1, leaves_dev + 1 + 2 * levels, 2)
    parent = slice(leaves_dev + 2, leaves_dev + 2 + 2 * levels, 2)
    transfer = jnp.einsum("tij,tkj->tik", upper[own], inverse[parent], precision=HIGHEST)[None]
    coupling = jnp.einsum("tij,tkj->tik", inverse[own], upper[sibling], precision=HIGHEST)[None]

    total_leaves = leaves_dev * lax.axis_size(("group", "sub"))
    first_leaf = lax.axis_index(("group", "sub")) * leaves_dev
    local = jnp.arange(leaves_dev, dtype=jnp.int32)[:, None]
    offsets = jnp.remainder(neighbours - first_leaf - local + reach, total_leaves) - reach
    picks = reach + local + offsets
    near_blocks = near_field(lower_parts + [leaves] + upper_parts, leaves, picks, beta)
    return (near_blocks, leaf_basis, transfer, coupling)


def solution(mesh):
    return jax.shard_map(
        shards,
        mesh=mesh,
        in_specs=(P(("group", "sub"), None), P(), P(("group", "sub"), None)),
        out_specs=(
            P(("group", "sub"), None, None),
            P(("group", "sub"), None),
            P(("group", "sub"), None, None, None),
            P(("group", "sub"), None, None, None),
        ),
        check_vma=False,
    )
```

```python
import functools
import math

import jax
import jax.numpy as jnp
from jax import lax
from jax.experimental import pallas as pl
from jax.experimental.pallas import tpu as pltpu
from jax.sharding import PartitionSpec as P

LEAF = 512
PANEL = 32
HIGHEST = lax.Precision.HIGHEST


def from_behind(value, axis, steps):
    count = lax.axis_size(axis)
    pairs = [(source, (source + steps) % count) for source in range(count)]
    return lax.ppermute(value, axis, pairs)


def from_partner(block, axis, stride):
    count = lax.axis_size(axis)
    route = []
    for low in range(count):
        high = low | 1 << stride
        if high != low and high < count:
            route += [(low, high), (high, low)]
    return lax.ppermute(block, axis, route)


def unit_rows(values):
    wide = values.astype(jnp.float32)
    scale = lax.rsqrt(jnp.sum(wide * wide, axis=-1, keepdims=True) + 1e-06)
    return (wide * scale).astype(jnp.bfloat16)


def split3(x):
    a = x.astype(jnp.bfloat16)
    rest = x - a.astype(jnp.float32)
    b = rest.astype(jnp.bfloat16)
    c = (rest - b.astype(jnp.float32)).astype(jnp.bfloat16)
    return a, b, c


def factor_kernel(count, rank, grams_ref, upper_ref, inverse_ref, work, *blocks):
    b = PANEL
    eye_row = lax.broadcasted_iota(jnp.int32, (rank, rank), 0)
    eye_col = lax.broadcasted_iota(jnp.int32, (rank, rank), 1)
    eye = jnp.where(eye_row == eye_col, 1.0, 0.0).astype(jnp.float32)
    for m in range(count):
        work[m, :, :rank] = grams_ref[m]
        work[m, :, rank:] = eye
    for block in blocks:
        block[...] = jnp.ones_like(block)
    lane = lax.broadcasted_iota(jnp.int32, (b, 128), 1)
    row = lax.broadcasted_iota(jnp.int32, (b, 128), 0)
    unit_part = jnp.where(lane == row + b, 1.0, 0.0).astype(jnp.float32)
    panel_row = lax.broadcasted_iota(jnp.int32, (b, rank), 0)
    panel_col = lax.broadcasted_iota(jnp.int32, (b, rank), 1)

    def panel(step, carry):
        start = pl.multiple_of(step * b, b)
        for m in range(count):
            rows = work[m, pl.ds(start, b), :rank]
            rolled = pltpu.roll(rows, rank - start, 1)[:, :128]
            blocks[m // 8][pl.ds(m % 8, b, stride=8), :] = jnp.where(lane < b, rolled, unit_part)
        for block in blocks:
            v = [block[r * 8:(r + 1) * 8, :] for r in range(b)]
            for k in range(b):
                pivot = jnp.broadcast_to(v[k][:, k:k + 1], (8, 128))
                scaled = v[k] * (1.0 / pivot)
                for i in range(k + 1, b):
                    v[i] = v[i] - jnp.broadcast_to(v[k][:, i:i + 1], (8, 128)) * scaled
                block[k * 8:(k + 1) * 8, :] = v[k] * lax.rsqrt(pivot)
        for m in range(count):
            small = blocks[m // 8][pl.ds(m % 8, b, stride=8), :][:, b:2 * b]
            reduced = jnp.dot(small, work[m, pl.ds(start, b), :], precision=HIGHEST, preferred_element_type=jnp.float32)
            left = jnp.where(panel_col >= start + panel_row, reduced[:, :rank], 0.0)
            work[m, pl.ds(start, b), :rank] = left
            work[m, pl.ds(start, b), rank:] = reduced[:, rank:]
            full = jnp.concatenate([left, reduced[:, rank:]], axis=1)
            y1, y2, y3 = split3(full)
            x1, x2, x3 = split3(jnp.where(panel_col >= start + b, left, 0.0))
            lhs = jnp.concatenate([x1, x1, x2, x2, x1, x3], axis=0)
            rhs = jnp.concatenate([y1, y2, y1, y2, y3, y1], axis=0)
            work[m] = work[m] - lax.dot_general(lhs, rhs, (((0,), (0,)), ((), ())), preferred_element_type=jnp.float32)
        return carry

    lax.fori_loop(0, rank // b, panel, 0)
    for m in range(count):
        upper_ref[m] = work[m, :, :rank]
        inverse_ref[m] = work[m, :, rank:]


def factors_of(grams):
    count, rank, _ = grams.shape
    shape = jax.ShapeDtypeStruct((count, rank, rank), jnp.float32)
    vmem = pl.BlockSpec(memory_space=pltpu.VMEM)
    return pl.pallas_call(
        functools.partial(factor_kernel, count, rank),
        out_shape=(shape, shape),
        in_specs=[vmem],
        out_specs=(vmem, vmem),
        scratch_shapes=[pltpu.VMEM((count, rank, 2 * rank), jnp.float32)]
        + [pltpu.VMEM((8 * PANEL, 128), jnp.float32)] * ((count + 7) // 8),
        compiler_params=pltpu.CompilerParams(vmem_limit_bytes=40 << 20),
        cost_estimate=pl.CostEstimate(flops=40_000_000_000, bytes_accessed=8_000_000, transcendentals=0),
        name="factor",
    )(grams)


def near_kernel(beta, picks_ref, *refs):
    *parts, rows_ref, out_ref, window, sems = refs
    leaf = pl.program_id(0)

    @pl.when((leaf == 0) & (pl.program_id(1) == 0))
    def _():
        at = 0
        copies = []
        for n, part in enumerate(parts):
            size = part.shape[0]
            copies.append(pltpu.make_async_copy(part, window.at[pl.ds(at, size)], sems.at[n]))
            at += size
        for copy in copies:
            copy.start()
        for copy in copies:
            copy.wait()

    rows = rows_ref[0]
    for j in range(out_ref.shape[1]):
        cols = window[picks_ref[leaf, j]]
        scores = lax.dot_general(rows, cols, (((1,), (1,)), ((), ())), preferred_element_type=jnp.float32)
        out_ref[:, j, :] = jnp.exp(beta * scores)


def near_field(parts, leaves, picks, beta):
    leaves_dev, leaf, width = leaves.shape
    nbr = picks.shape[1]
    chunk = 256
    steps = leaf // chunk
    total = sum(part.shape[0] for part in parts)
    return pl.pallas_call(
        functools.partial(near_kernel, beta),
        out_shape=jax.ShapeDtypeStruct((leaves_dev * leaf, nbr, leaf), jnp.float32),
        grid_spec=pltpu.PrefetchScalarGridSpec(
            num_scalar_prefetch=1,
            grid=(leaves_dev, steps),
            in_specs=[pl.BlockSpec(memory_space=pl.ANY)] * len(parts)
            + [pl.BlockSpec((1, chunk, width), lambda a, c, p: (a, c, 0))],
            out_specs=pl.BlockSpec((chunk, nbr, leaf), lambda a, c, p: (a * steps + c, 0, 0)),
            scratch_shapes=[
                pltpu.VMEM((total, leaf, width), jnp.bfloat16),
                pltpu.SemaphoreType.DMA((len(parts),)),
            ],
        ),
        compiler_params=pltpu.CompilerParams(vmem_limit_bytes=40 << 20),
        cost_estimate=pl.CostEstimate(flops=4_000_000_000, bytes_accessed=16_000_000, transcendentals=2_000_000),
        name="near",
    )(picks, *parts, leaves)


def shards(points, anchors, neighbours):
    leaves_dev = neighbours.shape[0]
    width = points.shape[1]
    rank = anchors.shape[0]
    beta = 0.5 * math.sqrt(width)
    unit = unit_rows(points)
    anchor_unit = unit_rows(anchors)
    leaves = unit.reshape(leaves_dev, LEAF, width)
    reach = 3
    plan = []
    for step in range(1, (reach + leaves_dev - 1) // leaves_dev + 1):
        count = min(leaves_dev, reach - (step - 1) * leaves_dev)
        plan.append((leaves[leaves_dev - count :], step))
        plan.append((leaves[:count], -step))
    sketch = jnp.exp(beta * jnp.dot(unit, anchor_unit.T, preferred_element_type=jnp.float32))
    sketch = sketch.reshape(leaves_dev, LEAF, rank)
    grams = jnp.einsum("lpr,lps->lrs", sketch, sketch, precision=HIGHEST) / LEAF
    node = jnp.sum(grams, axis=0) / leaves_dev
    levels = lax.axis_size("sub").bit_length() - 1
    stack = [grams[leaf] for leaf in range(leaves_dev)] + [node]
    for level in range(levels):
        partner = from_partner(node, "sub", level)
        node = (node + partner) * 0.5
        stack += [partner, node]
    held, stack = lax.optimization_barrier(([piece for piece, _ in plan], stack))
    got = {step: from_behind(piece, ("group", "sub"), step) for piece, (_, step) in zip(held, plan)}
    lower_parts = [got[step] for step in sorted(got, reverse=True) if step > 0]
    upper_parts = [got[step] for step in sorted(got, reverse=True) if step < 0]
    upper, inverse = factors_of(jnp.stack(stack, axis=0))
    basis = jnp.einsum("lpr,lsr->lps", sketch, inverse[:leaves_dev], precision=HIGHEST)
    leaf_basis = basis.reshape(leaves_dev * LEAF, rank).astype(jnp.bfloat16)
    own = slice(leaves_dev, leaves_dev + 2 * levels, 2)
    sibling = slice(leaves_dev + 1, leaves_dev + 1 + 2 * levels, 2)
    parent = slice(leaves_dev + 2, leaves_dev + 2 + 2 * levels, 2)
    transfer = jnp.einsum("tij,tkj->tik", upper[own], inverse[parent], precision=HIGHEST)[None]
    coupling = jnp.einsum("tij,tkj->tik", inverse[own], upper[sibling], precision=HIGHEST)[None]

    total_leaves = leaves_dev * lax.axis_size(("group", "sub"))
    first_leaf = lax.axis_index(("group", "sub")) * leaves_dev
    local = jnp.arange(leaves_dev, dtype=jnp.int32)[:, None]
    offsets = jnp.remainder(neighbours - first_leaf - local + reach, total_leaves) - reach
    picks = reach + local + offsets
    near_blocks = near_field(lower_parts + [leaves] + upper_parts, leaves, picks, beta)
    return (near_blocks, leaf_basis, transfer, coupling)


def solution(mesh):
    return jax.shard_map(
        shards,
        mesh=mesh,
        in_specs=(P(("group", "sub"), None), P(), P(("group", "sub"), None)),
        out_specs=(
            P(("group", "sub"), None, None),
            P(("group", "sub"), None),
            P(("group", "sub"), None, None, None),
            P(("group", "sub"), None, None, None),
        ),
        check_vma=False,
    )
```

```python
import functools
import math

import jax
import jax.numpy as jnp
from jax import lax
from jax.experimental import pallas as pl
from jax.experimental.pallas import tpu as pltpu
from jax.sharding import PartitionSpec as P

LEAF = 512
PANEL = 32
HIGHEST = lax.Precision.HIGHEST


def from_behind(value, axis, steps):
    count = lax.axis_size(axis)
    pairs = [(source, (source + steps) % count) for source in range(count)]
    return lax.ppermute(value, axis, pairs)


def unit_rows(values):
    wide = values.astype(jnp.float32)
    scale = lax.rsqrt(jnp.sum(wide * wide, axis=-1, keepdims=True) + 1e-06)
    return (wide * scale).astype(jnp.bfloat16)


def split3(x):
    a = x.astype(jnp.bfloat16)
    rest = x - a.astype(jnp.float32)
    b = rest.astype(jnp.bfloat16)
    c = (rest - b.astype(jnp.float32)).astype(jnp.bfloat16)
    return a, b, c


def factor_kernel(count, rank, grams_ref, upper_ref, inverse_ref, work, *blocks):
    b = PANEL
    eye_row = lax.broadcasted_iota(jnp.int32, (rank, rank), 0)
    eye_col = lax.broadcasted_iota(jnp.int32, (rank, rank), 1)
    eye = jnp.where(eye_row == eye_col, 1.0, 0.0).astype(jnp.float32)
    for m in range(count):
        work[m, :, :rank] = grams_ref[m]
        work[m, :, rank:] = eye
    for block in blocks:
        block[...] = jnp.ones_like(block)
    lane = lax.broadcasted_iota(jnp.int32, (b, 128), 1)
    row = lax.broadcasted_iota(jnp.int32, (b, 128), 0)
    unit_part = jnp.where(lane == row + b, 1.0, 0.0).astype(jnp.float32)
    panel_row = lax.broadcasted_iota(jnp.int32, (b, rank), 0)
    panel_col = lax.broadcasted_iota(jnp.int32, (b, rank), 1)

    def panel(step, carry):
        start = pl.multiple_of(step * b, b)
        for m in range(count):
            rows = work[m, pl.ds(start, b), :rank]
            rolled = pltpu.roll(rows, rank - start, 1)[:, :128]
            blocks[m // 8][pl.ds(m % 8, b, stride=8), :] = jnp.where(lane < b, rolled, unit_part)
        for block in blocks:
            v = [block[r * 8:(r + 1) * 8, :] for r in range(b)]
            for k in range(b):
                pivot = jnp.broadcast_to(v[k][:, k:k + 1], (8, 128))
                scaled = v[k] * (1.0 / pivot)
                for i in range(k + 1, b):
                    v[i] = v[i] - jnp.broadcast_to(v[k][:, i:i + 1], (8, 128)) * scaled
                block[k * 8:(k + 1) * 8, :] = v[k] * lax.rsqrt(pivot)
        for m in range(count):
            small = blocks[m // 8][pl.ds(m % 8, b, stride=8), :][:, b:2 * b]
            reduced = jnp.dot(small, work[m, pl.ds(start, b), :], precision=HIGHEST, preferred_element_type=jnp.float32)
            left = jnp.where(panel_col >= start + panel_row, reduced[:, :rank], 0.0)
            work[m, pl.ds(start, b), :rank] = left
            work[m, pl.ds(start, b), rank:] = reduced[:, rank:]
            full = jnp.concatenate([left, reduced[:, rank:]], axis=1)
            y1, y2, y3 = split3(full)
            x1, x2, x3 = split3(jnp.where(panel_col >= start + b, left, 0.0))
            lhs = jnp.concatenate([x1, x1, x2, x2, x1, x3], axis=0)
            rhs = jnp.concatenate([y1, y2, y1, y2, y3, y1], axis=0)
            work[m] = work[m] - lax.dot_general(lhs, rhs, (((0,), (0,)), ((), ())), preferred_element_type=jnp.float32)
        return carry

    lax.fori_loop(0, rank // b, panel, 0)
    for m in range(count):
        upper_ref[m] = work[m, :, :rank]
        inverse_ref[m] = work[m, :, rank:]


def factors_of(grams):
    count, rank, _ = grams.shape
    shape = jax.ShapeDtypeStruct((count, rank, rank), jnp.float32)
    vmem = pl.BlockSpec(memory_space=pltpu.VMEM)
    return pl.pallas_call(
        functools.partial(factor_kernel, count, rank),
        out_shape=(shape, shape),
        in_specs=[vmem],
        out_specs=(vmem, vmem),
        scratch_shapes=[pltpu.VMEM((count, rank, 2 * rank), jnp.float32)]
        + [pltpu.VMEM((8 * PANEL, 128), jnp.float32)] * ((count + 7) // 8),
        compiler_params=pltpu.CompilerParams(vmem_limit_bytes=40 << 20),
        cost_estimate=pl.CostEstimate(flops=40_000_000_000, bytes_accessed=8_000_000, transcendentals=0),
        name="factor",
    )(grams)


def near_kernel(beta, picks_ref, *refs):
    *parts, rows_ref, out_ref, window, sems = refs
    leaf = pl.program_id(0)

    @pl.when((leaf == 0) & (pl.program_id(1) == 0))
    def _():
        at = 0
        copies = []
        for n, part in enumerate(parts):
            size = part.shape[0]
            copies.append(pltpu.make_async_copy(part, window.at[pl.ds(at, size)], sems.at[n]))
            at += size
        for copy in copies:
            copy.start()
        for copy in copies:
            copy.wait()

    rows = rows_ref[0]
    for j in range(out_ref.shape[1]):
        cols = window[picks_ref[leaf, j]]
        scores = lax.dot_general(rows, cols, (((1,), (1,)), ((), ())), preferred_element_type=jnp.float32)
        out_ref[:, j, :] = jnp.exp(beta * scores)


def near_field(parts, leaves, picks, beta):
    leaves_dev, leaf, width = leaves.shape
    nbr = picks.shape[1]
    chunk = 256
    steps = leaf // chunk
    total = sum(part.shape[0] for part in parts)
    return pl.pallas_call(
        functools.partial(near_kernel, beta),
        out_shape=jax.ShapeDtypeStruct((leaves_dev * leaf, nbr, leaf), jnp.float32),
        grid_spec=pltpu.PrefetchScalarGridSpec(
            num_scalar_prefetch=1,
            grid=(leaves_dev, steps),
            in_specs=[pl.BlockSpec(memory_space=pl.ANY)] * len(parts)
            + [pl.BlockSpec((1, chunk, width), lambda a, c, p: (a, c, 0))],
            out_specs=pl.BlockSpec((chunk, nbr, leaf), lambda a, c, p: (a * steps + c, 0, 0)),
            scratch_shapes=[
                pltpu.VMEM((total, leaf, width), jnp.bfloat16),
                pltpu.SemaphoreType.DMA((len(parts),)),
            ],
        ),
        compiler_params=pltpu.CompilerParams(vmem_limit_bytes=40 << 20),
        cost_estimate=pl.CostEstimate(flops=4_000_000_000, bytes_accessed=16_000_000, transcendentals=2_000_000),
        name="near",
    )(picks, *parts, leaves)


def shards(points, anchors, neighbours):
    leaves_dev = neighbours.shape[0]
    width = points.shape[1]
    rank = anchors.shape[0]
    beta = 0.5 * math.sqrt(width)
    unit = unit_rows(points)
    anchor_unit = unit_rows(anchors)
    leaves = unit.reshape(leaves_dev, LEAF, width)
    reach = 3
    plan = []
    for step in range(1, (reach + leaves_dev - 1) // leaves_dev + 1):
        count = min(leaves_dev, reach - (step - 1) * leaves_dev)
        plan.append((leaves[leaves_dev - count :], step))
        plan.append((leaves[:count], -step))
    got = {step: from_behind(piece, ("group", "sub"), step) for piece, step in plan}
    sketch = jnp.exp(beta * jnp.dot(unit, anchor_unit.T, preferred_element_type=jnp.float32))
    sketch = sketch.reshape(leaves_dev, LEAF, rank)
    grams = jnp.einsum("lpr,lps->lrs", sketch, sketch, precision=HIGHEST) / LEAF
    node = jnp.sum(grams, axis=0) / leaves_dev
    levels = lax.axis_size("sub").bit_length() - 1
    mine = lax.axis_index("sub")
    stack = [grams[leaf] for leaf in range(leaves_dev)] + [node]
    nodes = lax.all_gather(node, "sub", axis=0)
    for level in range(levels):
        stack.append(lax.dynamic_index_in_dim(nodes, (mine >> level) ^ 1, 0, keepdims=False))
        nodes = (nodes[0::2] + nodes[1::2]) * 0.5
        stack.append(lax.dynamic_index_in_dim(nodes, mine >> (level + 1), 0, keepdims=False))
    lower_parts = [got[step] for step in sorted(got, reverse=True) if step > 0]
    upper_parts = [got[step] for step in sorted(got, reverse=True) if step < 0]
    upper, inverse = factors_of(jnp.stack(stack, axis=0))
    basis = jnp.einsum("lpr,lsr->lps", sketch, inverse[:leaves_dev], precision=HIGHEST)
    leaf_basis = basis.reshape(leaves_dev * LEAF, rank).astype(jnp.bfloat16)
    own = slice(leaves_dev, leaves_dev + 2 * levels, 2)
    sibling = slice(leaves_dev + 1, leaves_dev + 1 + 2 * levels, 2)
    parent = slice(leaves_dev + 2, leaves_dev + 2 + 2 * levels, 2)
    transfer = jnp.einsum("tij,tkj->tik", upper[own], inverse[parent], precision=HIGHEST)[None]
    coupling = jnp.einsum("tij,tkj->tik", inverse[own], upper[sibling], precision=HIGHEST)[None]

    total_leaves = leaves_dev * lax.axis_size(("group", "sub"))
    first_leaf = lax.axis_index(("group", "sub")) * leaves_dev
    local = jnp.arange(leaves_dev, dtype=jnp.int32)[:, None]
    offsets = jnp.remainder(neighbours - first_leaf - local + reach, total_leaves) - reach
    picks = reach + local + offsets
    near_blocks = near_field(lower_parts + [leaves] + upper_parts, leaves, picks, beta)
    return (near_blocks, leaf_basis, transfer, coupling)


def solution(mesh):
    return jax.shard_map(
        shards,
        mesh=mesh,
        in_specs=(P(("group", "sub"), None), P(), P(("group", "sub"), None)),
        out_specs=(
            P(("group", "sub"), None, None),
            P(("group", "sub"), None),
            P(("group", "sub"), None, None, None),
            P(("group", "sub"), None, None, None),
        ),
        check_vma=False,
    )
```

```python
import functools
import math

import jax
import jax.numpy as jnp
from jax import lax
from jax.experimental import pallas as pl
from jax.experimental.pallas import tpu as pltpu
from jax.sharding import PartitionSpec as P

LEAF = 512
PANEL = 32
HIGHEST = lax.Precision.HIGHEST


def from_behind(value, axis, steps):
    count = lax.axis_size(axis)
    pairs = [(source, (source + steps) % count) for source in range(count)]
    return lax.ppermute(value, axis, pairs)


def from_partner(block, axis, stride):
    count = lax.axis_size(axis)
    route = []
    for low in range(count):
        high = low | 1 << stride
        if high != low and high < count:
            route += [(low, high), (high, low)]
    return lax.ppermute(block, axis, route)


def unit_rows(values):
    wide = values.astype(jnp.float32)
    scale = lax.rsqrt(jnp.sum(wide * wide, axis=-1, keepdims=True) + 1e-06)
    return (wide * scale).astype(jnp.bfloat16)


def split3(x):
    a = x.astype(jnp.bfloat16)
    rest = x - a.astype(jnp.float32)
    b = rest.astype(jnp.bfloat16)
    c = (rest - b.astype(jnp.float32)).astype(jnp.bfloat16)
    return a, b, c


def factor_kernel(count, rank, grams_ref, upper_ref, inverse_ref, work, *blocks):
    b = PANEL
    eye_row = lax.broadcasted_iota(jnp.int32, (rank, rank), 0)
    eye_col = lax.broadcasted_iota(jnp.int32, (rank, rank), 1)
    eye = jnp.where(eye_row == eye_col, 1.0, 0.0).astype(jnp.float32)
    for m in range(count):
        work[m, :, :rank] = grams_ref[m]
        work[m, :, rank:] = eye
    for block in blocks:
        block[...] = jnp.ones_like(block)
    lane = lax.broadcasted_iota(jnp.int32, (b, 128), 1)
    row = lax.broadcasted_iota(jnp.int32, (b, 128), 0)
    unit_part = jnp.where(lane == row + b, 1.0, 0.0).astype(jnp.float32)
    panel_row = lax.broadcasted_iota(jnp.int32, (b, rank), 0)
    panel_col = lax.broadcasted_iota(jnp.int32, (b, rank), 1)

    def panel(step, carry):
        start = pl.multiple_of(step * b, b)
        for m in range(count):
            rows = work[m, pl.ds(start, b), :rank]
            rolled = pltpu.roll(rows, rank - start, 1)[:, :128]
            blocks[m // 8][pl.ds(m % 8, b, stride=8), :] = jnp.where(lane < b, rolled, unit_part)
        for block in blocks:
            v = [block[r * 8:(r + 1) * 8, :] for r in range(b)]
            for k in range(b):
                pivot = jnp.broadcast_to(v[k][:, k:k + 1], (8, 128))
                scaled = v[k] * (1.0 / pivot)
                for i in range(k + 1, b):
                    v[i] = v[i] - jnp.broadcast_to(v[k][:, i:i + 1], (8, 128)) * scaled
                block[k * 8:(k + 1) * 8, :] = v[k] * lax.rsqrt(pivot)
        for m in range(count):
            small = blocks[m // 8][pl.ds(m % 8, b, stride=8), :][:, b:2 * b]
            reduced = jnp.dot(small, work[m, pl.ds(start, b), :], precision=HIGHEST, preferred_element_type=jnp.float32)
            left = jnp.where(panel_col >= start + panel_row, reduced[:, :rank], 0.0)
            work[m, pl.ds(start, b), :rank] = left
            work[m, pl.ds(start, b), rank:] = reduced[:, rank:]
            full = jnp.concatenate([left, reduced[:, rank:]], axis=1)
            y1, y2, y3 = split3(full)
            x1, x2, x3 = split3(jnp.where(panel_col >= start + b, left, 0.0))
            lhs = jnp.concatenate([x1, x1, x2, x2, x1, x3], axis=0)
            rhs = jnp.concatenate([y1, y2, y1, y2, y3, y1], axis=0)
            work[m] = work[m] - lax.dot_general(lhs, rhs, (((0,), (0,)), ((), ())), preferred_element_type=jnp.float32)
        return carry

    lax.fori_loop(0, rank // b, panel, 0)
    for m in range(count):
        upper_ref[m] = work[m, :, :rank]
        inverse_ref[m] = work[m, :, rank:]


def factors_of(grams):
    count, rank, _ = grams.shape
    shape = jax.ShapeDtypeStruct((count, rank, rank), jnp.float32)
    vmem = pl.BlockSpec(memory_space=pltpu.VMEM)
    return pl.pallas_call(
        functools.partial(factor_kernel, count, rank),
        out_shape=(shape, shape),
        in_specs=[vmem],
        out_specs=(vmem, vmem),
        scratch_shapes=[pltpu.VMEM((count, rank, 2 * rank), jnp.float32)]
        + [pltpu.VMEM((8 * PANEL, 128), jnp.float32)] * ((count + 7) // 8),
        compiler_params=pltpu.CompilerParams(vmem_limit_bytes=40 << 20),
        cost_estimate=pl.CostEstimate(flops=40_000_000_000, bytes_accessed=8_000_000, transcendentals=0),
        name="factor",
    )(grams)


def near_kernel(beta, picks_ref, *refs):
    *parts, rows_ref, out_ref, window, sems = refs
    leaf = pl.program_id(0)

    @pl.when((leaf == 0) & (pl.program_id(1) == 0))
    def _():
        at = 0
        copies = []
        for n, part in enumerate(parts):
            size = part.shape[0]
            copies.append(pltpu.make_async_copy(part, window.at[pl.ds(at, size)], sems.at[n]))
            at += size
        for copy in copies:
            copy.start()
        for copy in copies:
            copy.wait()

    rows = rows_ref[0]
    for j in range(out_ref.shape[1]):
        cols = window[pl.ds(pl.multiple_of(picks_ref[leaf, j] * LEAF, LEAF), LEAF), :]
        scores = lax.dot_general(rows, cols, (((1,), (1,)), ((), ())), preferred_element_type=jnp.float32)
        out_ref[:, j, :] = jnp.exp(beta * scores)


def near_field(parts, leaves, picks, beta):
    leaves_dev, leaf, width = leaves.shape
    nbr = picks.shape[1]
    chunk = 256
    steps = leaf // chunk
    total = sum(part.shape[0] for part in parts)
    return pl.pallas_call(
        functools.partial(near_kernel, beta),
        out_shape=jax.ShapeDtypeStruct((leaves_dev * leaf, nbr, leaf), jnp.float32),
        grid_spec=pltpu.PrefetchScalarGridSpec(
            num_scalar_prefetch=1,
            grid=(leaves_dev, steps),
            in_specs=[pl.BlockSpec(memory_space=pl.ANY)] * len(parts)
            + [pl.BlockSpec((1, chunk, width), lambda a, c, p: (a, c, 0))],
            out_specs=pl.BlockSpec((chunk, nbr, leaf), lambda a, c, p: (a * steps + c, 0, 0)),
            scratch_shapes=[
                pltpu.VMEM((total, width), jnp.bfloat16),
                pltpu.SemaphoreType.DMA((len(parts),)),
            ],
        ),
        compiler_params=pltpu.CompilerParams(vmem_limit_bytes=40 << 20),
        cost_estimate=pl.CostEstimate(flops=4_000_000_000, bytes_accessed=16_000_000, transcendentals=2_000_000),
        name="near",
    )(picks, *parts, leaves)


def shards(points, anchors, neighbours):
    leaves_dev = neighbours.shape[0]
    width = points.shape[1]
    rank = anchors.shape[0]
    beta = 0.5 * math.sqrt(width)
    unit = unit_rows(points)
    anchor_unit = unit_rows(anchors)
    leaves = unit.reshape(leaves_dev, LEAF, width)
    reach = 3
    plan = []
    for step in range(1, (reach + leaves_dev - 1) // leaves_dev + 1):
        count = min(leaves_dev, reach - (step - 1) * leaves_dev)
        plan.append((leaves[leaves_dev - count :], step))
        plan.append((leaves[:count], -step))
    share = LEAF // 2
    first = {}
    late = []
    for piece, step in plan:
        piece = piece.reshape(-1, width)
        if abs(step) == 1:
            first[step] = from_behind(piece[:share], ("group", "sub"), step)
            piece = piece[share:]
        late.append((piece, step))
    sketch = jnp.exp(beta * jnp.dot(unit, anchor_unit.T, preferred_element_type=jnp.float32))
    sketch = sketch.reshape(leaves_dev, LEAF, rank)
    grams = jnp.einsum("lpr,lps->lrs", sketch, sketch, precision=HIGHEST) / LEAF
    node = jnp.sum(grams, axis=0) / leaves_dev
    levels = lax.axis_size("sub").bit_length() - 1
    stack = [grams[leaf] for leaf in range(leaves_dev)] + [node]
    for level in range(levels):
        partner = from_partner(node, "sub", level)
        node = (node + partner) * 0.5
        stack += [partner, node]
    held, stack, first = lax.optimization_barrier(([piece for piece, _ in late], stack, first))
    got = {step: [from_behind(piece, ("group", "sub"), step)] for piece, (_, step) in zip(held, late)}
    for step, piece in first.items():
        got[step].insert(0, piece)
    lower_parts = [piece for step in sorted(got, reverse=True) if step > 0 for piece in got[step]]
    upper_parts = [piece for step in sorted(got, reverse=True) if step < 0 for piece in got[step]]
    upper, inverse = factors_of(jnp.stack(stack, axis=0))
    basis = jnp.einsum("lpr,lsr->lps", sketch, inverse[:leaves_dev], precision=HIGHEST)
    leaf_basis = basis.reshape(leaves_dev * LEAF, rank).astype(jnp.bfloat16)
    own = slice(leaves_dev, leaves_dev + 2 * levels, 2)
    sibling = slice(leaves_dev + 1, leaves_dev + 1 + 2 * levels, 2)
    parent = slice(leaves_dev + 2, leaves_dev + 2 + 2 * levels, 2)
    transfer = jnp.einsum("tij,tkj->tik", upper[own], inverse[parent], precision=HIGHEST)[None]
    coupling = jnp.einsum("tij,tkj->tik", inverse[own], upper[sibling], precision=HIGHEST)[None]

    total_leaves = leaves_dev * lax.axis_size(("group", "sub"))
    first_leaf = lax.axis_index(("group", "sub")) * leaves_dev
    local = jnp.arange(leaves_dev, dtype=jnp.int32)[:, None]
    offsets = jnp.remainder(neighbours - first_leaf - local + reach, total_leaves) - reach
    picks = reach + local + offsets
    near_blocks = near_field(lower_parts + [unit] + upper_parts, leaves, picks, beta)
    return (near_blocks, leaf_basis, transfer, coupling)


def solution(mesh):
    return jax.shard_map(
        shards,
        mesh=mesh,
        in_specs=(P(("group", "sub"), None), P(), P(("group", "sub"), None)),
        out_specs=(
            P(("group", "sub"), None, None),
            P(("group", "sub"), None),
            P(("group", "sub"), None, None, None),
            P(("group", "sub"), None, None, None),
        ),
        check_vma=False,
    )
```

```python
import functools
import math

import jax
import jax.numpy as jnp
from jax import lax
from jax.experimental import pallas as pl
from jax.experimental.pallas import tpu as pltpu
from jax.sharding import PartitionSpec as P

LEAF = 512
PANEL = 32
HIGHEST = lax.Precision.HIGHEST


def from_behind(value, axis, steps):
    count = lax.axis_size(axis)
    pairs = [(source, (source + steps) % count) for source in range(count)]
    return lax.ppermute(value, axis, pairs)


def from_partner(block, axis, stride):
    count = lax.axis_size(axis)
    route = []
    for low in range(count):
        high = low | 1 << stride
        if high != low and high < count:
            route += [(low, high), (high, low)]
    return lax.ppermute(block, axis, route)


def unit_rows(values):
    wide = values.astype(jnp.float32)
    scale = lax.rsqrt(jnp.sum(wide * wide, axis=-1, keepdims=True) + 1e-06)
    return (wide * scale).astype(jnp.bfloat16)


def split3(x):
    a = x.astype(jnp.bfloat16)
    rest = x - a.astype(jnp.float32)
    b = rest.astype(jnp.bfloat16)
    c = (rest - b.astype(jnp.float32)).astype(jnp.bfloat16)
    return a, b, c


def factor_kernel(count, rank, grams_ref, upper_ref, inverse_ref, work, *blocks):
    b = PANEL
    for m in range(count):
        work[m] = grams_ref[m]
    for block in blocks:
        block[...] = jnp.ones_like(block)
    lane = lax.broadcasted_iota(jnp.int32, (b, 128), 1)
    row = lax.broadcasted_iota(jnp.int32, (b, 128), 0)
    unit_part = jnp.where(lane == row + b, 1.0, 0.0).astype(jnp.float32)
    panel_row = lax.broadcasted_iota(jnp.int32, (b, rank), 0)
    panel_col = lax.broadcasted_iota(jnp.int32, (b, rank), 1)

    all_col = lax.broadcasted_iota(jnp.int32, (rank, rank), 1)

    def panel(step, carry):
        start = pl.multiple_of(step * b, b)
        for m in range(count):
            rows = work[m, pl.ds(start, b), :]
            rolled = pltpu.roll(rows, rank - start, 1)[:, :128]
            blocks[m // 8][pl.ds(m % 8, b, stride=8), :] = jnp.where(lane < b, rolled, unit_part)
        for block in blocks:
            v = [block[r * 8:(r + 1) * 8, :] for r in range(b)]
            for k in range(b):
                pivot = jnp.broadcast_to(v[k][:, k:k + 1], (8, 128))
                scaled = v[k] * (1.0 / pivot)
                for i in range(k + 1, b):
                    v[i] = v[i] - jnp.broadcast_to(v[k][:, i:i + 1], (8, 128)) * scaled
                block[k * 8:(k + 1) * 8, :] = v[k] * lax.rsqrt(pivot)
        for m in range(count):
            strip = blocks[m // 8][pl.ds(m % 8, b, stride=8), :]
            small = strip[:, b:2 * b]
            reduced = jnp.dot(small, work[m, pl.ds(start, b), :], precision=HIGHEST, preferred_element_type=jnp.float32)
            left = jnp.where(panel_col >= start + panel_row, reduced, 0.0)
            upper_ref[m, pl.ds(start, b), :] = left
            placed = pltpu.roll(jnp.concatenate([strip] + [jnp.zeros_like(strip)] * (rank // 128 - 1), axis=1), lax.rem(start + rank - b, rank), 1)
            done = jnp.where(panel_col < start, reduced, jnp.where(panel_col <= start + panel_row, placed, 0.0))
            inverse_ref[m, pl.ds(start, b), :] = done
            full = jnp.where(panel_col < start + b, done, reduced)
            y1, y2, y3 = split3(full)
            x1, x2, x3 = split3(jnp.where(panel_col >= start + b, reduced, 0.0))
            lhs = jnp.concatenate([x1, x1, x2, x2, x1, x3], axis=0)
            rhs = jnp.concatenate([y1, y2, y1, y2, y3, y1], axis=0)
            kept = jnp.where((all_col >= start) & (all_col < start + b), 0.0, work[m])
            work[m] = kept - lax.dot_general(lhs, rhs, (((0,), (0,)), ((), ())), preferred_element_type=jnp.float32)
        return carry

    lax.fori_loop(0, rank // b, panel, 0)


def factors_of(grams):
    count, rank, _ = grams.shape
    shape = jax.ShapeDtypeStruct((count, rank, rank), jnp.float32)
    vmem = pl.BlockSpec(memory_space=pltpu.VMEM)
    return pl.pallas_call(
        functools.partial(factor_kernel, count, rank),
        out_shape=(shape, shape),
        in_specs=[vmem],
        out_specs=(vmem, vmem),
        scratch_shapes=[pltpu.VMEM((count, rank, rank), jnp.float32)]
        + [pltpu.VMEM((8 * PANEL, 128), jnp.float32)] * ((count + 7) // 8),
        compiler_params=pltpu.CompilerParams(vmem_limit_bytes=40 << 20),
        cost_estimate=pl.CostEstimate(flops=40_000_000_000, bytes_accessed=8_000_000, transcendentals=0),
        name="factor",
    )(grams)


def near_kernel(beta, picks_ref, *refs):
    *parts, rows_ref, out_ref, window, sems = refs
    leaf = pl.program_id(0)

    @pl.when((leaf == 0) & (pl.program_id(1) == 0))
    def _():
        at = 0
        copies = []
        for n, part in enumerate(parts):
            size = part.shape[0]
            copies.append(pltpu.make_async_copy(part, window.at[pl.ds(at, size)], sems.at[n]))
            at += size
        for copy in copies:
            copy.start()
        for copy in copies:
            copy.wait()

    rows = rows_ref[0]
    for j in range(out_ref.shape[1]):
        cols = window[pl.ds(pl.multiple_of(picks_ref[leaf, j] * LEAF, LEAF), LEAF), :]
        scores = lax.dot_general(rows, cols, (((1,), (1,)), ((), ())), preferred_element_type=jnp.float32)
        out_ref[:, j, :] = jnp.exp(beta * scores)


def near_field(parts, leaves, picks, beta):
    leaves_dev, leaf, width = leaves.shape
    nbr = picks.shape[1]
    chunk = 256
    steps = leaf // chunk
    total = sum(part.shape[0] for part in parts)
    return pl.pallas_call(
        functools.partial(near_kernel, beta),
        out_shape=jax.ShapeDtypeStruct((leaves_dev * leaf, nbr, leaf), jnp.float32),
        grid_spec=pltpu.PrefetchScalarGridSpec(
            num_scalar_prefetch=1,
            grid=(leaves_dev, steps),
            in_specs=[pl.BlockSpec(memory_space=pl.ANY)] * len(parts)
            + [pl.BlockSpec((1, chunk, width), lambda a, c, p: (a, c, 0))],
            out_specs=pl.BlockSpec((chunk, nbr, leaf), lambda a, c, p: (a * steps + c, 0, 0)),
            scratch_shapes=[
                pltpu.VMEM((total, width), jnp.bfloat16),
                pltpu.SemaphoreType.DMA((len(parts),)),
            ],
        ),
        compiler_params=pltpu.CompilerParams(vmem_limit_bytes=40 << 20),
        cost_estimate=pl.CostEstimate(flops=4_000_000_000, bytes_accessed=16_000_000, transcendentals=2_000_000),
        name="near",
    )(picks, *parts, leaves)


def shards(points, anchors, neighbours):
    leaves_dev = neighbours.shape[0]
    width = points.shape[1]
    rank = anchors.shape[0]
    beta = 0.5 * math.sqrt(width)
    unit = unit_rows(points)
    anchor_unit = unit_rows(anchors)
    leaves = unit.reshape(leaves_dev, LEAF, width)
    reach = 3
    plan = []
    for step in range(1, (reach + leaves_dev - 1) // leaves_dev + 1):
        count = min(leaves_dev, reach - (step - 1) * leaves_dev)
        plan.append((leaves[leaves_dev - count :], step))
        plan.append((leaves[:count], -step))
    share = LEAF * 3 // 8
    first = {}
    late = []
    for piece, step in plan:
        piece = piece.reshape(-1, width)
        if abs(step) == 1:
            first[step] = from_behind(piece[:share], ("group", "sub"), step)
            piece = piece[share:]
        late.append((piece, step))
    sketch = jnp.exp(beta * jnp.dot(unit, anchor_unit.T, preferred_element_type=jnp.float32))
    sketch = sketch.reshape(leaves_dev, LEAF, rank)
    grams = jnp.einsum("lpr,lps->lrs", sketch, sketch, precision=HIGHEST) / LEAF
    node = jnp.sum(grams, axis=0) / leaves_dev
    levels = lax.axis_size("sub").bit_length() - 1
    stack = [grams[leaf] for leaf in range(leaves_dev)] + [node]
    for level in range(levels):
        partner = from_partner(node, "sub", level)
        node = (node + partner) * 0.5
        stack += [partner, node]
    held, stack, first = lax.optimization_barrier(([piece for piece, _ in late], stack, first))
    got = {step: [from_behind(piece, ("group", "sub"), step)] for piece, (_, step) in zip(held, late)}
    for step, piece in first.items():
        got[step].insert(0, piece)
    lower_parts = [piece for step in sorted(got, reverse=True) if step > 0 for piece in got[step]]
    upper_parts = [piece for step in sorted(got, reverse=True) if step < 0 for piece in got[step]]
    upper, inverse = factors_of(jnp.stack(stack, axis=0))
    basis = jnp.einsum("lpr,lsr->lps", sketch, inverse[:leaves_dev], precision=HIGHEST)
    leaf_basis = basis.reshape(leaves_dev * LEAF, rank).astype(jnp.bfloat16)
    own = slice(leaves_dev, leaves_dev + 2 * levels, 2)
    sibling = slice(leaves_dev + 1, leaves_dev + 1 + 2 * levels, 2)
    parent = slice(leaves_dev + 2, leaves_dev + 2 + 2 * levels, 2)
    transfer = jnp.einsum("tij,tkj->tik", upper[own], inverse[parent], precision=HIGHEST)[None]
    coupling = jnp.einsum("tij,tkj->tik", inverse[own], upper[sibling], precision=HIGHEST)[None]

    total_leaves = leaves_dev * lax.axis_size(("group", "sub"))
    first_leaf = lax.axis_index(("group", "sub")) * leaves_dev
    local = jnp.arange(leaves_dev, dtype=jnp.int32)[:, None]
    offsets = jnp.remainder(neighbours - first_leaf - local + reach, total_leaves) - reach
    picks = reach + local + offsets
    near_blocks = near_field(lower_parts + [unit] + upper_parts, leaves, picks, beta)
    return (near_blocks, leaf_basis, transfer, coupling)


def solution(mesh):
    return jax.shard_map(
        shards,
        mesh=mesh,
        in_specs=(P(("group", "sub"), None), P(), P(("group", "sub"), None)),
        out_specs=(
            P(("group", "sub"), None, None),
            P(("group", "sub"), None),
            P(("group", "sub"), None, None, None),
            P(("group", "sub"), None, None, None),
        ),
        check_vma=False,
    )
```
